32 devices in a mesh: group: 2 (over x), blk: 8 (over z, y), uly: 2 (over core).
Axes of the slice: x: 2, y: 2, z: 4, core: 2. Of those that a mesh axis runs over, the one named last changes fastest.
Arguments:
- queries: bfloat16 [4096, 4096], P(('group', 'blk', 'uly')), parts along dimension 0, may hold values from -6 to 6
- key_states: bfloat16 [4096, 1024], P(('group', 'blk', 'uly')), parts along dimension 0, may hold values from -6 to 6
- value_states: bfloat16 [4096, 1024], P(('group', 'blk', 'uly')), parts along dimension 0, may hold values from -6 to 6
- out_grad: bfloat16 [4096, 4096], P(('group', 'blk', 'uly')), parts along dimension 0, may hold values from -6 to 6
- pattern: int32 [32, 8], replicated, may hold values from 0 to 31, as said below
Outputs:
- attended: bfloat16 [4096, 4096], P(('group', 'blk', 'uly')), parts along dimension 0
- query_grad: bfloat16 [4096, 4096], P(('group', 'blk', 'uly')), parts along dimension 0
- key_grad: bfloat16 [4096, 1024], P(('group', 'blk', 'uly')), parts along dimension 0
- value_grad: bfloat16 [4096, 1024], P(('group', 'blk', 'uly')), parts along dimension 0
The draws below stay inside these ranges and needn't reach their ends.
There are 2 independent parts, one for each index of `group`. The reference program is written for one: setup_inputs(seed, part) draws one part's arguments, and reference() takes and returns one part's arrays. A program takes and returns all parts, laid end to end along the dimension named above; an argument that names none is the same for every part. Nothing has to cross between parts.
Inputs may be any that keep to these rules, and one draw needn't show every extreme that they name: `pattern`: columns 0 to 2 of row i are i - 1, i, i + 1 modulo 32; columns 3 and 4 are 0 and 31; the last 3 columns are random blocks. Take the rows s * 4 to (s + 1) * 4 - 1 of one group s and count each listed block once: the blocks of any other group r (blocks r * 4 to (r + 1) * 4 - 1) number at most 2, and exactly 2 for some other group of every group.
All inputs are finite; a program needn't handle non-finite values.
Results may differ from the reference program's by a relative error of at most 0.024.
Values may be sent and summed in bfloat16 or wider, within the bound.
A program may use at most 128 MiB of HBM per device.

```python
import jax
import jax.numpy as jnp
from jax import lax

H = 32
KVH = 8
HD = 128
BLOCK = 64
RAND = 3
CAP = 2
KB = 8
SEQ = 2048
NB = 32
QB = 4
N_BLK = 8


def drawn_pair(key):
    query_key = jax.random.fold_in(key, 11)
    keys_key = jax.random.fold_in(key, 12)
    query_draw = jnp.clip(jax.random.normal(query_key, (SEQ, H * HD), jnp.float32), -6.0, 6.0)
    keys_draw = jnp.clip(jax.random.normal(keys_key, (SEQ, KVH * HD), jnp.float32), -6.0, 6.0)
    return (query_draw, keys_draw)


def draw_queries(key, part):
    return drawn_pair(key)[0].astype(jnp.bfloat16)


def draw_key_states(key, part):
    return drawn_pair(key)[1].astype(jnp.bfloat16)


def draw_pattern(key, part):
    shards = N_BLK
    keys_list = jax.random.split(key, 5)
    shard_ids = jnp.arange(shards, dtype=jnp.int32)
    popular = jax.random.randint(keys_list[0], (shards,), 0, 5, dtype=jnp.int32)
    coins = jax.random.randint(keys_list[1], (shards, shards), 0, 4, dtype=jnp.int32)
    others = (coins < popular[None, :]).astype(jnp.int32)
    hottest = (shard_ids + jax.random.randint(keys_list[2], (shards,), 1, shards, dtype=jnp.int32)) % shards
    fixed_blocks = jnp.stack([(shard_ids * QB - 1) % NB, (shard_ids + 1) * QB % NB, jnp.zeros((shards,), jnp.int32), jnp.full((shards,), NB - 1, jnp.int32)], axis=1)
    owners = fixed_blocks // QB
    fresh_cols = [jnp.ones((shards,), jnp.bool_)]
    for column in range(1, 4):
        fresh_cols.append(jnp.logical_not(jnp.any(fixed_blocks[:, :column] == fixed_blocks[:, column:column + 1], axis=1)))
    fresh = jnp.stack(fresh_cols, axis=1)
    structural = jnp.zeros((shards, shards), jnp.int32)
    for column in range(4):
        counted = fresh[:, column, None] & (owners[:, column, None] == shard_ids[None, :]) & (owners[:, column, None] != shard_ids[:, None])
        structural = structural + counted.astype(jnp.int32)
    room = CAP - structural
    counts = jnp.where(shard_ids[None, :] == hottest[:, None], room, jnp.minimum(1 + others, room))
    counts = jnp.maximum(jnp.where(shard_ids[None, :] == shard_ids[:, None], 0, counts), 0)
    inner = QB - 2
    inner_ids = jnp.arange(inner, dtype=jnp.int32)
    ranking = jax.random.randint(keys_list[3], (shards, shards, inner), 0, 1 << 20, dtype=jnp.int32) * inner + inner_ids
    ordering = jnp.argsort(ranking, axis=-1).astype(jnp.int32)
    candidates = shard_ids[None, :, None] * QB + 1 + ordering
    picked = inner_ids[None, None, :] < counts[:, :, None]
    total_cand = shards * inner
    flat_cand = candidates.reshape(shards, total_cand)
    flat_picked = picked.reshape(shards, total_cand)
    cand_owner = jnp.arange(total_cand, dtype=jnp.int32) // inner
    is_hot = cand_owner[None, :] == hottest[:, None]
    tier = jnp.where(flat_picked, jnp.where(is_hot, 0, 1), 2)
    sort_keys = tier * total_cand + jnp.arange(total_cand, dtype=jnp.int32)[None, :]
    arranged = jnp.take_along_axis(flat_cand, jnp.argsort(sort_keys, axis=1).astype(jnp.int32), axis=1)
    chosen_count = jnp.maximum(jnp.sum(flat_picked.astype(jnp.int32), axis=1), 1)
    slots_total = QB * RAND
    spots = jnp.arange(slots_total, dtype=jnp.int32)
    source_spot = jnp.where(spots[None, :] < chosen_count[:, None], spots[None, :], spots[None, :] % chosen_count[:, None])
    randoms = jnp.take_along_axis(arranged, source_spot, axis=1)
    mixing = jax.random.randint(keys_list[4], (shards, slots_total), 0, 1 << 20, dtype=jnp.int32) * slots_total + spots[None, :]
    randoms = jnp.take_along_axis(randoms, jnp.argsort(mixing, axis=1).astype(jnp.int32), axis=1)
    randoms = randoms.reshape(NB, RAND)
    blocks = jnp.arange(NB, dtype=jnp.int32)
    window = jnp.stack([(blocks - 1) % NB, blocks, (blocks + 1) % NB, jnp.zeros((NB,), jnp.int32), jnp.full((NB,), NB - 1, jnp.int32)], axis=1)
    return jnp.concatenate([window, randoms], axis=1).astype(jnp.int32)


def shard_levels(rng, shape, cuts, least, largest):
    factor_of = 1.0
    for axis_at, parts in cuts:
        draws = jax.random.uniform(jax.random.fold_in(jax.random.fold_in(rng, 6), axis_at), (parts,), jnp.float32, least / len(cuts), largest / len(cuts))
        factor_of = factor_of * jnp.repeat(jnp.exp(draws), shape[axis_at] // parts).reshape((-1,) + (1,) * (len(shape) - 1 - axis_at))
    return factor_of


def centred(key, dims, deviation, bound, cuts=(), kind=jnp.bfloat16):
    entries = jax.random.normal(key, dims, jnp.float32) * deviation
    if len(cuts) > 0:
        entries = shard_levels(key, dims, cuts, -0.22, 0.18) * entries
    return jnp.clip(entries, min=-bound, max=bound).astype(kind)


def setup_inputs(seed: int = 0, part: int = 0) -> dict:
    seeds = jax.random.split(jax.random.key(seed), 6)
    part_splits = jax.random.split(jax.random.fold_in(seeds[5], part), 6)
    return {
        "queries": draw_queries(jax.random.fold_in(jax.random.fold_in(seeds[5], part), 71), part),
        "key_states": draw_key_states(jax.random.fold_in(jax.random.fold_in(seeds[5], part), 71), part),
        "value_states": centred(part_splits[2], (SEQ, KVH * HD), 1.0, 6.0, ((0, 16),)),
        "out_grad": centred(part_splits[3], (SEQ, H * HD), 1.0, 6.0, ((0, 16),)),
        "pattern": draw_pattern(jax.random.fold_in(seeds[5], 71), part),
    }


def reference(queries, key_states, value_states, out_grad, pattern):
    repeat = H // KVH
    softmax_scale = HD ** -0.5
    key_blocks = key_states.reshape(NB, BLOCK, KVH, HD)
    value_blocks = value_states.reshape(NB, BLOCK, KVH, HD)

    def one_shard(totals, shard):
        key_total, value_total = totals
        listed_ids = lax.dynamic_slice_in_dim(pattern, shard * QB, QB, 0).reshape(-1).astype(jnp.int32)
        first_row = (shard * QB * BLOCK).astype(jnp.int32)
        query_part = lax.dynamic_slice_in_dim(queries, first_row, QB * BLOCK, 0).astype(jnp.float32).reshape(QB, BLOCK, KVH, repeat, HD)
        grad_part = lax.dynamic_slice_in_dim(out_grad, first_row, QB * BLOCK, 0).astype(jnp.float32).reshape(QB, BLOCK, KVH, repeat, HD)
        listed_keys = key_blocks[listed_ids].astype(jnp.float32).reshape(QB, KB * BLOCK, KVH, HD)
        listed_values = value_blocks[listed_ids].astype(jnp.float32).reshape(QB, KB * BLOCK, KVH, HD)
        scores = jnp.einsum("qbgrd,qkgd->qgrbk", query_part, listed_keys) * softmax_scale
        shifted = jnp.exp(scores - jnp.max(scores, axis=-1, keepdims=True))
        probs = shifted / jnp.sum(shifted, axis=-1, keepdims=True)
        probs_low = lax.optimization_barrier(probs.astype(jnp.bfloat16)).astype(jnp.float32)
        attended_low = lax.optimization_barrier(jnp.einsum("qgrbk,qkgd->qbgrd", probs_low, listed_values).astype(jnp.bfloat16))
        attended_wide = attended_low.astype(jnp.float32)
        delta = jnp.einsum("qbgrd,qbgrd->qgrb", grad_part, attended_wide)
        dprobs = jnp.einsum("qbgrd,qkgd->qgrbk", grad_part, listed_values)
        dscores = probs * (dprobs - delta[..., None])
        dscores_low = lax.optimization_barrier(dscores.astype(jnp.bfloat16)).astype(jnp.float32)
        query_grad = (jnp.einsum("qgrbk,qkgd->qbgrd", dscores_low, listed_keys) * softmax_scale).astype(jnp.bfloat16)
        key_part = jnp.einsum("qgrbk,qbgrd->qkgd", dscores_low, query_part) * softmax_scale
        value_part = jnp.einsum("qgrbk,qbgrd->qkgd", probs_low, grad_part)
        key_part = key_part.reshape(QB * KB, BLOCK, KVH * HD)
        value_part = value_part.reshape(QB * KB, BLOCK, KVH * HD)
        key_shard = jnp.zeros((NB, BLOCK, KVH * HD), jnp.float32).at[listed_ids].add(key_part)
        value_shard = jnp.zeros((NB, BLOCK, KVH * HD), jnp.float32).at[listed_ids].add(value_part)
        key_total = key_total + lax.optimization_barrier(key_shard.astype(jnp.bfloat16)).astype(jnp.float32)
        value_total = value_total + lax.optimization_barrier(value_shard.astype(jnp.bfloat16)).astype(jnp.float32)
        return (key_total, value_total), (attended_low.reshape(QB * BLOCK, H * HD), query_grad.reshape(QB * BLOCK, H * HD))

    start_totals = (jnp.zeros((NB, BLOCK, KVH * HD), jnp.float32), jnp.zeros((NB, BLOCK, KVH * HD), jnp.float32))
    totals, stacked = lax.scan(one_shard, start_totals, jnp.arange(N_BLK, dtype=jnp.int32))
    attended = stacked[0].reshape(SEQ, H * HD)
    query_grad = stacked[1].reshape(SEQ, H * HD)
    key_grad = totals[0].astype(jnp.bfloat16).reshape(SEQ, KVH * HD)
    value_grad = totals[1].astype(jnp.bfloat16).reshape(SEQ, KVH * HD)
    return (attended, query_grad, key_grad, value_grad)
```

```python
import functools
import math

import jax
import jax.numpy as jnp
from jax import lax
from jax.experimental import pallas as pl
from jax.experimental.pallas import tpu as pltpu
from jax.sharding import PartitionSpec as P

HD = 128
BLOCK = 64
CAP = 2


def dot(a, b, dims):
    return lax.dot_general(a, b, (dims, ((), ())), preferred_element_type=jnp.float32)


def attend(
    repeat, qb, kb, rows_ref, pool_ref, q_ref, do_ref, k_ref, v_ref,
    att_ref, dq_ref, grad_ref, kl, vl, acc_k, acc_v,
):
    scale = HD ** (-0.5)
    acc_k[...] = jnp.zeros_like(acc_k)
    acc_v[...] = jnp.zeros_like(acc_v)
    for i in range(qb):
        tokens = pl.ds(i * BLOCK, BLOCK)
        for c in range(kb):
            row = pl.multiple_of(rows_ref[i * kb + c] * BLOCK, BLOCK)
            kl[pl.ds(c * BLOCK, BLOCK), :] = k_ref[pl.ds(row, BLOCK), :]
            vl[pl.ds(c * BLOCK, BLOCK), :] = v_ref[pl.ds(row, BLOCK), :]
        q = jnp.concatenate([q_ref[tokens, r * HD:(r + 1) * HD] for r in range(repeat)], axis=0)
        do = jnp.concatenate([do_ref[tokens, r * HD:(r + 1) * HD] for r in range(repeat)], axis=0)
        k = kl[...]
        v = vl[...]
        s = dot(k, q, ((1,), (1,))) * (scale * math.log2(math.e))
        e = jnp.exp2(s - jnp.max(s, axis=0, keepdims=True))
        p = e * (1.0 / jnp.sum(e, axis=0, keepdims=True))
        p_low = p.astype(jnp.bfloat16)
        att = dot(v, p_low, ((0,), (0,))).astype(jnp.bfloat16)
        do_t = jnp.transpose(do.astype(jnp.float32))
        delta = jnp.sum(do_t * att.astype(jnp.float32), axis=0, keepdims=True)
        dp = dot(v, do, ((1,), (1,)))
        ds_low = (p * (dp - delta)).astype(jnp.bfloat16)
        dq = dot(k, ds_low, ((0,), (0,))) * scale
        dk = dot(ds_low, q, ((1,), (0,))) * scale
        dv = dot(p_low, do, ((1,), (0,)))
        att_n = jnp.transpose(att.astype(jnp.float32)).astype(jnp.bfloat16)
        dq_n = jnp.transpose(dq).astype(jnp.bfloat16)
        for r in range(repeat):
            att_ref[tokens, r * HD:(r + 1) * HD] = att_n[r * BLOCK:(r + 1) * BLOCK]
            dq_ref[tokens, r * HD:(r + 1) * HD] = dq_n[r * BLOCK:(r + 1) * BLOCK]
        for c in range(kb):
            at = pl.ds(pl.multiple_of(pool_ref[i * kb + c] * BLOCK, BLOCK), BLOCK)
            acc_k[at, :] += dk[c * BLOCK:(c + 1) * BLOCK]
            acc_v[at, :] += dv[c * BLOCK:(c + 1) * BLOCK]
    grad_ref[0] = acc_k[...].astype(jnp.bfloat16)
    grad_ref[1] = acc_v[...].astype(jnp.bfloat16)


def attend_call(rows, pool, q, do, kv, qb, kb, pool_size):
    tokens, width = q.shape
    kv_rows, kv2 = kv.shape
    groups = kv2 // 2 // HD
    cols = width // groups
    q_spec = pl.BlockSpec((tokens, cols), lambda g, *_: (0, g))
    pr = pool_size * BLOCK
    return pl.pallas_call(
        functools.partial(attend, cols // HD, qb, kb),
        out_shape=(
            jax.ShapeDtypeStruct((tokens, width), jnp.bfloat16),
            jax.ShapeDtypeStruct((tokens, width), jnp.bfloat16),
            jax.ShapeDtypeStruct((2, pr, kv2 // 2), jnp.bfloat16),
        ),
        grid_spec=pltpu.PrefetchScalarGridSpec(
            num_scalar_prefetch=2,
            grid=(groups,),
            in_specs=[
                q_spec,
                q_spec,
                pl.BlockSpec((kv_rows, HD), lambda g, *_: (0, g)),
                pl.BlockSpec((kv_rows, HD), lambda g, *_: (0, groups + g)),
            ],
            out_specs=[q_spec, q_spec, pl.BlockSpec((2, pr, HD), lambda g, *_: (0, 0, g))],
            scratch_shapes=[
                pltpu.VMEM((kb * BLOCK, HD), jnp.bfloat16),
                pltpu.VMEM((kb * BLOCK, HD), jnp.bfloat16),
                pltpu.VMEM((pr, HD), jnp.float32),
                pltpu.VMEM((pr, HD), jnp.float32),
            ],
        ),
        compiler_params=pltpu.CompilerParams(vmem_limit_bytes=40 * 1024 * 1024),
        name="attend",
    )(rows, pool, q, do, kv, kv)


def combine(shards, qb, asked_ref, rank_ref, own_ref, back_ref, out_ref):
    for l in range(qb):
        out_rows = pl.ds(l * BLOCK, BLOCK)
        total = own_ref[0, out_rows, :].astype(jnp.float32)
        for d in range(shards):
            row = pl.multiple_of(rank_ref[d * qb + l] * BLOCK, BLOCK)
            term = back_ref[d, 0, pl.ds(row, BLOCK), :].astype(jnp.float32)
            total = total + jnp.where(asked_ref[d * qb + l] > 0, term, 0.0)
        out_ref[0, out_rows, :] = total.astype(jnp.bfloat16)


def combine_call(asked, rank, grads, back, qb):
    shards = back.shape[0]
    width = back.shape[-1]
    return pl.pallas_call(
        functools.partial(combine, shards, qb),
        out_shape=jax.ShapeDtypeStruct((2, qb * BLOCK, width), jnp.bfloat16),
        grid_spec=pltpu.PrefetchScalarGridSpec(
            num_scalar_prefetch=2,
            grid=(2,),
            in_specs=[
                pl.BlockSpec((1, qb * BLOCK, width), lambda t, *_: (t, 0, 0)),
                pl.BlockSpec((shards, 1, CAP * BLOCK, width), lambda t, *_: (0, t, 0, 0)),
            ],
            out_specs=pl.BlockSpec((1, qb * BLOCK, width), lambda t, *_: (t, 0, 0)),
        ),
        compiler_params=pltpu.CompilerParams(vmem_limit_bytes=40 * 1024 * 1024),
        name="combine",
    )(asked, rank, grads, back)


def plan(pattern, position, shards, qb):
    blocks, kb = pattern.shape
    ids = jnp.arange(blocks, dtype=jnp.int32)
    owner = ids // qb
    per_shard = pattern.reshape(shards, qb * kb)
    listed = jnp.any(per_shard[:, :, None] == ids[None, None, :], axis=1).astype(jnp.int32)
    before = ((owner[:, None] == owner[None, :]) & (ids[:, None] < ids[None, :])).astype(jnp.int32)
    rank_all = jnp.sum(listed[:, :, None] * before[None], axis=1)
    mine = lax.dynamic_slice_in_dim(per_shard, position, 1, 0).reshape(-1)
    my_rank = lax.dynamic_slice_in_dim(rank_all, position, 1, 0)
    rank = jnp.sum(jnp.where(mine[:, None] == ids[None, :], my_rank, 0), axis=1)
    pool = jnp.where(mine // qb == position, mine % qb, qb + (mine // qb) * CAP + rank)
    others = jnp.arange(shards, dtype=jnp.int32)[:, None] != position
    asked = lax.dynamic_slice_in_dim(listed, position * qb, qb, 1) * others
    asked_rank = jnp.where(asked > 0, lax.dynamic_slice_in_dim(rank_all, position * qb, qb, 1), 0)
    return mine, pool, asked.reshape(-1), asked_rank.reshape(-1)


def on_device(queries, key_states, value_states, out_grad, pattern):
    shards = lax.axis_size("blk")
    position = lax.axis_index("blk")
    swap = functools.partial(lax.all_to_all, axis_name="uly", split_axis=1, concat_axis=0, tiled=True)
    unswap = functools.partial(lax.all_to_all, axis_name="uly", split_axis=0, concat_axis=1, tiled=True)
    k, v = swap(key_states), swap(value_states)
    everything = lax.all_gather(jnp.concatenate([k, v], axis=1), "blk", axis=0, tiled=True)
    q, do = swap(queries), swap(out_grad)
    qb = q.shape[0] // BLOCK
    kb = pattern.shape[1]
    rows, pool, asked, rank = plan(pattern, position, shards, qb)
    att, dq, grads = attend_call(rows, pool, q, do, everything, qb, kb, qb + shards * CAP)
    width = grads.shape[-1]
    sent = grads[:, qb * BLOCK:].reshape(2, shards, CAP * BLOCK, width).transpose(1, 0, 2, 3)
    back = lax.all_to_all(sent, "blk", split_axis=0, concat_axis=0, tiled=True)
    kv_grad = combine_call(asked, rank, grads, back, qb)
    return unswap(att), unswap(dq), unswap(kv_grad[0]), unswap(kv_grad[1])


def solution(mesh):
    split = P(("group", "blk", "uly"), None)
    return jax.shard_map(
        on_device,
        mesh=mesh,
        in_specs=(split, split, split, split, P()),
        out_specs=(split, split, split, split),
        check_vma=False,
    )
```

```python
import functools
import math

import jax
import jax.numpy as jnp
from jax import lax
from jax.experimental import pallas as pl
from jax.experimental.pallas import tpu as pltpu
from jax.sharding import PartitionSpec as P

HD = 128
BLOCK = 64
CAP = 2


def dot(a, b, dims):
    return lax.dot_general(a, b, (dims, ((), ())), preferred_element_type=jnp.float32)


def attend(
    repeat, qb, kb, rows_ref, pool_ref, q_ref, do_ref, k_ref, v_ref,
    att_ref, dq_ref, grad_ref, kl, vl, acc_k, acc_v,
):
    scale = HD ** (-0.5)
    acc_k[...] = jnp.zeros_like(acc_k)
    acc_v[...] = jnp.zeros_like(acc_v)
    for i in range(qb):
        tokens = pl.ds(i * BLOCK, BLOCK)
        for c in range(kb):
            row = pl.multiple_of(rows_ref[i * kb + c] * BLOCK, BLOCK)
            kl[pl.ds(c * BLOCK, BLOCK), :] = k_ref[pl.ds(row, BLOCK), :]
            vl[pl.ds(c * BLOCK, BLOCK), :] = v_ref[pl.ds(row, BLOCK), :]
        q = jnp.concatenate([q_ref[tokens, r * HD:(r + 1) * HD] for r in range(repeat)], axis=0)
        do = jnp.concatenate([do_ref[tokens, r * HD:(r + 1) * HD] for r in range(repeat)], axis=0)
        k = kl[...]
        v = vl[...]
        s = dot(k, q, ((1,), (1,))) * (scale * math.log2(math.e))
        e = jnp.exp2(s - jnp.max(s, axis=0, keepdims=True))
        p = e * (1.0 / jnp.sum(e, axis=0, keepdims=True))
        p_low = p.astype(jnp.bfloat16)
        att = dot(v, p_low, ((0,), (0,))).astype(jnp.bfloat16)
        do_t = jnp.transpose(do.astype(jnp.float32))
        delta = jnp.sum(do_t * att.astype(jnp.float32), axis=0, keepdims=True)
        dp = dot(v, do, ((1,), (1,)))
        ds_low = (p * (dp - delta)).astype(jnp.bfloat16)
        dq = dot(k, ds_low, ((0,), (0,))) * scale
        dk = dot(ds_low, q, ((1,), (0,))) * scale
        dv = dot(p_low, do, ((1,), (0,)))
        att_n = jnp.transpose(att.astype(jnp.float32)).astype(jnp.bfloat16)
        dq_n = jnp.transpose(dq).astype(jnp.bfloat16)
        for r in range(repeat):
            att_ref[tokens, r * HD:(r + 1) * HD] = att_n[r * BLOCK:(r + 1) * BLOCK]
            dq_ref[tokens, r * HD:(r + 1) * HD] = dq_n[r * BLOCK:(r + 1) * BLOCK]
        for c in range(kb):
            at = pl.ds(pl.multiple_of(pool_ref[i * kb + c] * BLOCK, BLOCK), BLOCK)
            acc_k[at, :] += dk[c * BLOCK:(c + 1) * BLOCK]
            acc_v[at, :] += dv[c * BLOCK:(c + 1) * BLOCK]
    grad_ref[0] = acc_k[...].astype(jnp.bfloat16)
    grad_ref[1] = acc_v[...].astype(jnp.bfloat16)


def attend_call(rows, pool, q, do, kv, qb, kb, pool_size):
    tokens, width = q.shape
    kv_rows, kv2 = kv.shape
    groups = kv2 // 2 // HD
    cols = width // groups
    q_spec = pl.BlockSpec((tokens, cols), lambda g, *_: (0, g))
    pr = pool_size * BLOCK
    return pl.pallas_call(
        functools.partial(attend, cols // HD, qb, kb),
        out_shape=(
            jax.ShapeDtypeStruct((tokens, width), jnp.bfloat16),
            jax.ShapeDtypeStruct((tokens, width), jnp.bfloat16),
            jax.ShapeDtypeStruct((2, pr, kv2 // 2), jnp.bfloat16),
        ),
        grid_spec=pltpu.PrefetchScalarGridSpec(
            num_scalar_prefetch=2,
            grid=(groups,),
            in_specs=[
                q_spec,
                q_spec,
                pl.BlockSpec((kv_rows, HD), lambda g, *_: (0, g)),
                pl.BlockSpec((kv_rows, HD), lambda g, *_: (0, groups + g)),
            ],
            out_specs=[q_spec, q_spec, pl.BlockSpec((2, pr, HD), lambda g, *_: (0, 0, g))],
            scratch_shapes=[
                pltpu.VMEM((kb * BLOCK, HD), jnp.bfloat16),
                pltpu.VMEM((kb * BLOCK, HD), jnp.bfloat16),
                pltpu.VMEM((pr, HD), jnp.float32),
                pltpu.VMEM((pr, HD), jnp.float32),
            ],
        ),
        compiler_params=pltpu.CompilerParams(vmem_limit_bytes=40 * 1024 * 1024),
        name="attend",
    )(rows, pool, q, do, kv, kv)


MESH = pl.DeviceIdType.MESH
ANY = pl.BlockSpec(memory_space=pl.ANY)
SMEM = pl.BlockSpec(memory_space=pltpu.SMEM)


def part(index, size):
    return pl.ds(pl.multiple_of(index * size, size), size)


def greet(shards, me, mate):
    barrier = pltpu.get_barrier_semaphore()
    pl.semaphore_signal(barrier, inc=1, device_id={"uly": mate}, device_id_type=MESH)

    def one(o, carry):
        pl.semaphore_signal(
            barrier, inc=1, device_id={"blk": lax.rem(me + o, shards)}, device_id_type=MESH
        )
        return carry

    lax.fori_loop(1, shards, one, 0)
    pl.semaphore_wait(barrier, shards)


def to_mate(src, dst, sems, at, mate):
    return pltpu.make_async_remote_copy(
        src_ref=src, dst_ref=dst, send_sem=sems.at[0, at], recv_sem=sems.at[1, at],
        device_id={"uly": mate}, device_id_type=MESH,
    )


def bring(
    shards, qb, idx_ref, q_ref, do_ref, k_ref, v_ref, qh_ref, doh_ref, pool_ref,
    kv, out, local, mate_sems, blk_sems,
):
    me = lax.axis_index("blk")
    core = lax.axis_index("uly")
    mate = 1 - core
    rows, width = q_ref.shape
    half, kv_half = width // 2, k_ref.shape[1] // 2
    here = part(core, rows)
    first = pl.ds(0, kv_half)
    second = pl.ds(kv_half, kv_half)
    greet(shards, me, mate)
    ks = to_mate(k_ref.at[:, part(mate, kv_half)], kv.at[here, first], mate_sems, 0, mate)
    vs = to_mate(v_ref.at[:, part(mate, kv_half)], kv.at[here, second], mate_sems, 1, mate)
    ks.start()
    vs.start()
    kl = pltpu.make_async_copy(k_ref.at[:, part(core, kv_half)], kv.at[here, first], local.at[0])
    vl = pltpu.make_async_copy(v_ref.at[:, part(core, kv_half)], kv.at[here, second], local.at[1])
    kl.start()
    vl.start()
    kl.wait()
    vl.wait()
    ks.wait()
    vs.wait()

    def send(o):
        return pltpu.make_async_remote_copy(
            src_ref=out.at[o - 1],
            dst_ref=pool_ref.at[pl.ds(pl.multiple_of((qb + me * CAP) * BLOCK, BLOCK), CAP * BLOCK), :],
            send_sem=blk_sems.at[0, o - 1],
            recv_sem=blk_sems.at[1, o - 1],
            device_id={"blk": lax.rem(me + o, shards)},
            device_id_type=MESH,
        )

    def pack(o, carry):
        to = lax.rem(me + o, shards)
        for s in range(CAP):
            which = idx_ref[to * CAP + s]
            block = kv[0:BLOCK, :]
            for b in range(1, qb):
                block = jnp.where(which == b, kv[b * BLOCK:(b + 1) * BLOCK, :], block)
            out[o - 1, s * BLOCK:(s + 1) * BLOCK, :] = block
        send(o).start()
        return carry

    lax.fori_loop(1, shards, pack, 0)
    own = pltpu.make_async_copy(kv, pool_ref.at[pl.ds(0, qb * BLOCK), :], local.at[0])
    own.start()
    qs = to_mate(q_ref.at[:, part(mate, half)], qh_ref.at[here, :], mate_sems, 2, mate)
    ds = to_mate(do_ref.at[:, part(mate, half)], doh_ref.at[here, :], mate_sems, 3, mate)
    qs.start()
    ds.start()
    ql = pltpu.make_async_copy(q_ref.at[:, part(core, half)], qh_ref.at[here, :], local.at[1])
    dl = pltpu.make_async_copy(do_ref.at[:, part(core, half)], doh_ref.at[here, :], local.at[2])
    ql.start()
    dl.start()
    own.wait()
    ql.wait()
    dl.wait()
    qs.wait()
    ds.wait()

    def finish(o, carry):
        send(o).wait()
        return carry

    lax.fori_loop(1, shards, finish, 0)


def bring_call(idx, q, do, k, v, shards, qb, pool_size):
    rows, width = q.shape
    kv_width = k.shape[1]
    heads = jax.ShapeDtypeStruct((2 * rows, width // 2), q.dtype)
    return pl.pallas_call(
        functools.partial(bring, shards, qb),
        out_shape=(heads, heads, jax.ShapeDtypeStruct((pool_size * BLOCK, kv_width), k.dtype)),
        in_specs=[SMEM, ANY, ANY, ANY, ANY],
        out_specs=(ANY, ANY, ANY),
        scratch_shapes=[
            pltpu.VMEM((qb * BLOCK, kv_width), k.dtype),
            pltpu.VMEM((shards - 1, CAP * BLOCK, kv_width), k.dtype),
            pltpu.SemaphoreType.DMA((3,)),
            pltpu.SemaphoreType.DMA((2, 4)),
            pltpu.SemaphoreType.DMA((2, shards - 1)),
        ],
        compiler_params=pltpu.CompilerParams(
            collective_id=0, has_side_effects=True, vmem_limit_bytes=40 * 1024 * 1024
        ),
        name="bring",
    )(idx, q, do, k, v)


def give(
    shards, qb, sel_ref, att_ref, dq_ref, grad_ref, atto_ref, dqo_ref, dko_ref, dvo_ref,
    own, back, total, done, local, mate_sems, blk_sems,
):
    me = lax.axis_index("blk")
    core = lax.axis_index("uly")
    mate = 1 - core
    rows, width = atto_ref.shape
    half, kv_half = width // 2, dko_ref.shape[1] // 2
    greet(shards, me, mate)

    def send(o):
        to = lax.rem(me + o, shards)
        return pltpu.make_async_remote_copy(
            src_ref=grad_ref.at[:, pl.ds(pl.multiple_of((qb + to * CAP) * BLOCK, BLOCK), CAP * BLOCK), :],
            dst_ref=back.at[o - 1],
            send_sem=blk_sems.at[0, o - 1],
            recv_sem=blk_sems.at[1, o - 1],
            device_id={"blk": to},
            device_id_type=MESH,
        )

    def start(o, carry):
        send(o).start()
        return carry

    lax.fori_loop(1, shards, start, 0)
    mine = pltpu.make_async_copy(grad_ref.at[:, pl.ds(0, qb * BLOCK), :], own, local.at[0])
    mine.start()
    there = part(core, half)
    ats = to_mate(att_ref.at[part(mate, rows), :], atto_ref.at[:, there], mate_sems, 0, mate)
    dqs = to_mate(dq_ref.at[part(mate, rows), :], dqo_ref.at[:, there], mate_sems, 1, mate)
    ats.start()
    dqs.start()
    atl = pltpu.make_async_copy(att_ref.at[part(core, rows), :], atto_ref.at[:, there], local.at[1])
    dql = pltpu.make_async_copy(dq_ref.at[part(core, rows), :], dqo_ref.at[:, there], local.at[2])
    atl.start()
    dql.start()
    mine.wait()
    total[...] = own[...].astype(jnp.float32)

    def add(o, carry):
        send(o).wait()
        source = lax.rem(me - o + shards, shards)
        for l in range(qb):
            lo = l * BLOCK
            pick = sel_ref[source * qb + l]
            for t in range(2):
                term = total[t, lo:lo + BLOCK, :]
                for s in range(CAP):
                    piece = back[o - 1, t, s * BLOCK:(s + 1) * BLOCK, :].astype(jnp.float32)
                    term = term + jnp.where(pick == s, piece, 0.0)
                total[t, lo:lo + BLOCK, :] = term
        return carry

    lax.fori_loop(1, shards, add, 0)
    done[...] = total[...].astype(done.dtype)
    kv_there = part(core, kv_half)
    kvs = []
    for t, ref in enumerate((dko_ref, dvo_ref)):
        kvs.append(to_mate(done.at[t, part(mate, rows), :], ref.at[:, kv_there], mate_sems, 2 + t, mate))
        kvs.append(pltpu.make_async_copy(done.at[t, part(core, rows), :], ref.at[:, kv_there], local.at[3 + t]))
    for copy in kvs:
        copy.start()
    ats.wait()
    dqs.wait()
    atl.wait()
    dql.wait()
    for copy in kvs:
        copy.wait()


def give_call(sel, att, dq, grads, shards, qb):
    tokens, half = att.shape
    rows, kv_half = tokens // 2, grads.shape[2]
    wide = jax.ShapeDtypeStruct((rows, 2 * half), att.dtype)
    narrow = jax.ShapeDtypeStruct((rows, 2 * kv_half), att.dtype)
    return pl.pallas_call(
        functools.partial(give, shards, qb),
        out_shape=(wide, wide, narrow, narrow),
        in_specs=[SMEM, ANY, ANY, ANY],
        out_specs=(ANY, ANY, ANY, ANY),
        scratch_shapes=[
            pltpu.VMEM((2, qb * BLOCK, kv_half), jnp.bfloat16),
            pltpu.VMEM((shards - 1, 2, CAP * BLOCK, kv_half), jnp.bfloat16),
            pltpu.VMEM((2, qb * BLOCK, kv_half), jnp.float32),
            pltpu.VMEM((2, qb * BLOCK, kv_half), jnp.bfloat16),
            pltpu.SemaphoreType.DMA((5,)),
            pltpu.SemaphoreType.DMA((2, 4)),
            pltpu.SemaphoreType.DMA((2, shards - 1)),
        ],
        compiler_params=pltpu.CompilerParams(
            collective_id=1, has_side_effects=True, vmem_limit_bytes=40 * 1024 * 1024
        ),
        name="give",
    )(sel, att, dq, grads)


def plan(pattern, position, shards, qb):
    blocks, kb = pattern.shape
    ids = jnp.arange(blocks, dtype=jnp.int32)
    owner = ids // qb
    per_shard = pattern.reshape(shards, qb * kb)
    listed = jnp.any(per_shard[:, :, None] == ids[None, None, :], axis=1).astype(jnp.int32)
    before = ((owner[:, None] == owner[None, :]) & (ids[:, None] < ids[None, :])).astype(jnp.int32)
    rank_all = jnp.sum(listed[:, :, None] * before[None], axis=1)
    mine = lax.dynamic_slice_in_dim(per_shard, position, 1, 0).reshape(-1)
    my_rank = lax.dynamic_slice_in_dim(rank_all, position, 1, 0)
    rank = jnp.sum(jnp.where(mine[:, None] == ids[None, :], my_rank, 0), axis=1)
    pool = jnp.where(mine // qb == position, mine % qb, qb + (mine // qb) * CAP + rank)
    others = jnp.arange(shards, dtype=jnp.int32)[:, None] != position
    asked = lax.dynamic_slice_in_dim(listed, position * qb, qb, 1) * others
    asked_rank = lax.dynamic_slice_in_dim(rank_all, position * qb, qb, 1)
    pick = jnp.where(asked > 0, asked_rank, -1)
    slots = jnp.arange(CAP, dtype=jnp.int32)
    within = jnp.arange(qb, dtype=jnp.int32)
    idx = jnp.sum(jnp.where(pick[:, None, :] == slots[None, :, None], within, 0), axis=2)
    return pool, idx.reshape(-1), pick.reshape(-1)


def on_device(queries, key_states, value_states, out_grad, pattern):
    shards = lax.axis_size("blk")
    position = lax.axis_index("blk")
    qb = 2 * queries.shape[0] // BLOCK
    kb = pattern.shape[1]
    pool_size = qb + shards * CAP
    pool, idx, pick = plan(pattern, position, shards, qb)
    q, do, kv = bring_call(idx, queries, out_grad, key_states, value_states, shards, qb, pool_size)
    att, dq, grads = attend_call(pool, pool, q, do, kv, qb, kb, pool_size)
    return give_call(pick, att, dq, grads, shards, qb)


def solution(mesh):
    split = P(("group", "blk", "uly"), None)
    return jax.shard_map(
        on_device,
        mesh=mesh,
        in_specs=(split, split, split, split, P()),
        out_specs=(split, split, split, split),
        check_vma=False,
    )
```

```python
import functools
import math

import jax
import jax.numpy as jnp
from jax import lax
from jax.experimental import pallas as pl
from jax.experimental.pallas import tpu as pltpu
from jax.sharding import PartitionSpec as P

HD = 128
BLOCK = 64
CAP = 2


def dot(a, b, dims):
    return lax.dot_general(a, b, (dims, ((), ())), preferred_element_type=jnp.float32)


def attend(
    repeat, qb, kb, rows_ref, pool_ref, q_ref, do_ref, k_ref, v_ref,
    att_ref, dq_ref, grad_ref, kl, vl, acc_k, acc_v,
):
    scale = HD ** (-0.5)
    acc_k[...] = jnp.zeros_like(acc_k)
    acc_v[...] = jnp.zeros_like(acc_v)
    for i in range(qb):
        tokens = pl.ds(i * BLOCK, BLOCK)
        for c in range(kb):
            row = pl.multiple_of(rows_ref[i * kb + c] * BLOCK, BLOCK)
            kl[pl.ds(c * BLOCK, BLOCK), :] = k_ref[pl.ds(row, BLOCK), :]
            vl[pl.ds(c * BLOCK, BLOCK), :] = v_ref[pl.ds(row, BLOCK), :]
        q = jnp.concatenate([q_ref[tokens, r * HD:(r + 1) * HD] for r in range(repeat)], axis=0)
        do = jnp.concatenate([do_ref[tokens, r * HD:(r + 1) * HD] for r in range(repeat)], axis=0)
        k = kl[...]
        v = vl[...]
        s = dot(k, q, ((1,), (1,))) * (scale * math.log2(math.e))
        e = jnp.exp2(s - jnp.max(s, axis=0, keepdims=True))
        p = e * (1.0 / jnp.sum(e, axis=0, keepdims=True))
        p_low = p.astype(jnp.bfloat16)
        att = dot(v, p_low, ((0,), (0,))).astype(jnp.bfloat16)
        do_t = jnp.transpose(do.astype(jnp.float32))
        delta = jnp.sum(do_t * att.astype(jnp.float32), axis=0, keepdims=True)
        dp = dot(v, do, ((1,), (1,)))
        ds_low = (p * (dp - delta)).astype(jnp.bfloat16)
        dq = dot(k, ds_low, ((0,), (0,))) * scale
        dk = dot(ds_low, q, ((1,), (0,))) * scale
        dv = dot(p_low, do, ((1,), (0,)))
        att_n = jnp.transpose(att.astype(jnp.float32)).astype(jnp.bfloat16)
        dq_n = jnp.transpose(dq).astype(jnp.bfloat16)
        for r in range(repeat):
            att_ref[tokens, r * HD:(r + 1) * HD] = att_n[r * BLOCK:(r + 1) * BLOCK]
            dq_ref[tokens, r * HD:(r + 1) * HD] = dq_n[r * BLOCK:(r + 1) * BLOCK]
        for c in range(kb):
            at = pl.ds(pl.multiple_of(pool_ref[i * kb + c] * BLOCK, BLOCK), BLOCK)
            acc_k[at, :] += dk[c * BLOCK:(c + 1) * BLOCK]
            acc_v[at, :] += dv[c * BLOCK:(c + 1) * BLOCK]
    grad_ref[0] = acc_k[...].astype(jnp.bfloat16)
    grad_ref[1] = acc_v[...].astype(jnp.bfloat16)


def attend_call(rows, pool, q, do, kv, qb, kb, pool_size):
    tokens, width = q.shape
    kv_rows, kv2 = kv.shape
    groups = kv2 // 2 // HD
    cols = width // groups
    q_spec = pl.BlockSpec((tokens, cols), lambda g, *_: (0, g))
    pr = pool_size * BLOCK
    return pl.pallas_call(
        functools.partial(attend, cols // HD, qb, kb),
        out_shape=(
            jax.ShapeDtypeStruct((tokens, width), jnp.bfloat16),
            jax.ShapeDtypeStruct((tokens, width), jnp.bfloat16),
            jax.ShapeDtypeStruct((2, pr, kv2 // 2), jnp.bfloat16),
        ),
        grid_spec=pltpu.PrefetchScalarGridSpec(
            num_scalar_prefetch=2,
            grid=(groups,),
            in_specs=[
                q_spec,
                q_spec,
                pl.BlockSpec((kv_rows, HD), lambda g, *_: (0, g)),
                pl.BlockSpec((kv_rows, HD), lambda g, *_: (0, groups + g)),
            ],
            out_specs=[q_spec, q_spec, pl.BlockSpec((2, pr, HD), lambda g, *_: (0, 0, g))],
            scratch_shapes=[
                pltpu.VMEM((kb * BLOCK, HD), jnp.bfloat16),
                pltpu.VMEM((kb * BLOCK, HD), jnp.bfloat16),
                pltpu.VMEM((pr, HD), jnp.float32),
                pltpu.VMEM((pr, HD), jnp.float32),
            ],
        ),
        compiler_params=pltpu.CompilerParams(vmem_limit_bytes=40 * 1024 * 1024),
        name="attend",
    )(rows, pool, q, do, kv, kv)


MESH = pl.DeviceIdType.MESH
ANY = pl.BlockSpec(memory_space=pl.ANY)
SMEM = pl.BlockSpec(memory_space=pltpu.SMEM)


def part(index, size):
    return pl.ds(pl.multiple_of(index * size, size), size)


def greet(shards, me, mate):
    barrier = pltpu.get_barrier_semaphore()
    pl.semaphore_signal(barrier, inc=1, device_id={"uly": mate}, device_id_type=MESH)

    def one(o, carry):
        pl.semaphore_signal(
            barrier, inc=1, device_id={"blk": lax.rem(me + o, shards)}, device_id_type=MESH
        )
        return carry

    lax.fori_loop(1, shards, one, 0)
    pl.semaphore_wait(barrier, shards)


def to_mate(src, dst, sems, at, mate):
    return pltpu.make_async_remote_copy(
        src_ref=src, dst_ref=dst, send_sem=sems.at[0, at], recv_sem=sems.at[1, at],
        device_id={"uly": mate}, device_id_type=MESH,
    )


def bring(
    shards, qb, idx_ref, q_ref, do_ref, k_ref, v_ref, qh_ref, doh_ref, pool_ref,
    kv, far, out, local, mate_sems, twin_sems, blk_sems,
):
    me = lax.axis_index("blk")
    core = lax.axis_index("uly")
    mate = 1 - core
    rows, width = q_ref.shape
    half, kv_half = width // 2, k_ref.shape[1] // 2
    here = part(core, rows)
    first = pl.ds(0, kv_half)
    second = pl.ds(kv_half, kv_half)
    greet(shards, me, mate)
    ks = to_mate(k_ref.at[:, part(mate, kv_half)], kv.at[here, first], mate_sems, 0, mate)
    vs = to_mate(v_ref.at[:, part(mate, kv_half)], kv.at[here, second], mate_sems, 1, mate)
    ks.start()
    vs.start()
    kl = pltpu.make_async_copy(k_ref.at[:, part(core, kv_half)], kv.at[here, first], local.at[0])
    vl = pltpu.make_async_copy(v_ref.at[:, part(core, kv_half)], kv.at[here, second], local.at[1])
    kl.start()
    vl.start()
    kl.wait()
    vl.wait()
    ks.wait()
    vs.wait()

    half_size = shards // 2
    base = me // half_size * half_size
    place = lax.rem(me, half_size)
    twin = lax.rem(me + half_size, shards)
    halves = (first, second)

    def relay(t):
        return pltpu.make_async_remote_copy(
            src_ref=kv.at[:, halves[t]],
            dst_ref=far.at[:, halves[t]],
            send_sem=twin_sems.at[0, t],
            recv_sem=twin_sems.at[1, t],
            device_id={"blk": twin},
            device_id_type=MESH,
        )

    def send(f, t, o):
        owner = twin if f else me
        return pltpu.make_async_remote_copy(
            src_ref=out.at[f, o, :, halves[t]],
            dst_ref=pool_ref.at[
                pl.ds(pl.multiple_of((qb + owner * CAP) * BLOCK, BLOCK), CAP * BLOCK), halves[t]
            ],
            send_sem=blk_sems.at[0, f, t, o],
            recv_sem=blk_sems.at[1, f, t, o],
            device_id={"blk": base + lax.rem(place + o, half_size)},
            device_id_type=MESH,
        )

    def pack(source, f, t, o):
        to = base + lax.rem(place + o, half_size)
        for s in range(CAP):
            which = idx_ref[(f * shards + to) * CAP + s]
            block = source[0:BLOCK, halves[t]]
            for b in range(1, qb):
                block = jnp.where(which == b, source[b * BLOCK:(b + 1) * BLOCK, halves[t]], block)
            out[f, o, s * BLOCK:(s + 1) * BLOCK, halves[t]] = block

    relay(0).start()
    relay(1).start()

    def near(o, carry):
        for t in range(2):
            pack(kv, 0, t, o)
            send(0, t, o).start()
        return carry

    lax.fori_loop(1, half_size, near, 0)
    own = pltpu.make_async_copy(kv, pool_ref.at[pl.ds(0, qb * BLOCK), :], local.at[0])
    own.start()
    qs = to_mate(q_ref.at[:, part(mate, half)], qh_ref.at[here, :], mate_sems, 2, mate)
    ds = to_mate(do_ref.at[:, part(mate, half)], doh_ref.at[here, :], mate_sems, 3, mate)
    qs.start()
    ds.start()
    ql = pltpu.make_async_copy(q_ref.at[:, part(core, half)], qh_ref.at[here, :], local.at[1])
    dl = pltpu.make_async_copy(do_ref.at[:, part(core, half)], doh_ref.at[here, :], local.at[2])
    ql.start()
    dl.start()
    for t in range(2):
        relay(t).wait()

        def onward(o, carry):
            pack(far, 1, t, o)
            send(1, t, o).start()
            return carry

        lax.fori_loop(1, half_size, onward, 0)
        pack(far, 1, t, 0)
    kept = pltpu.make_async_copy(
        out.at[1, 0],
        pool_ref.at[pl.ds(pl.multiple_of((qb + twin * CAP) * BLOCK, BLOCK), CAP * BLOCK), :],
        local.at[3],
    )
    kept.start()
    own.wait()
    ql.wait()
    dl.wait()
    qs.wait()
    ds.wait()
    kept.wait()

    def finish(o, carry):
        for f in range(2):
            for t in range(2):
                send(f, t, o).wait()
        return carry

    lax.fori_loop(1, half_size, finish, 0)


def bring_call(idx, q, do, k, v, shards, qb, pool_size):
    rows, width = q.shape
    kv_width = k.shape[1]
    heads = jax.ShapeDtypeStruct((2 * rows, width // 2), q.dtype)
    return pl.pallas_call(
        functools.partial(bring, shards, qb),
        out_shape=(heads, heads, jax.ShapeDtypeStruct((pool_size * BLOCK, kv_width), k.dtype)),
        in_specs=[SMEM, ANY, ANY, ANY, ANY],
        out_specs=(ANY, ANY, ANY),
        scratch_shapes=[
            pltpu.VMEM((qb * BLOCK, kv_width), k.dtype),
            pltpu.VMEM((qb * BLOCK, kv_width), k.dtype),
            pltpu.VMEM((2, shards // 2, CAP * BLOCK, kv_width), k.dtype),
            pltpu.SemaphoreType.DMA((4,)),
            pltpu.SemaphoreType.DMA((2, 4)),
            pltpu.SemaphoreType.DMA((2, 2)),
            pltpu.SemaphoreType.DMA((2, 2, 2, shards // 2)),
        ],
        compiler_params=pltpu.CompilerParams(
            collective_id=0, has_side_effects=True, vmem_limit_bytes=56 * 1024 * 1024
        ),
        name="bring",
    )(idx, q, do, k, v)


def give(
    shards, qb, sel_ref, att_ref, dq_ref, grad_ref, atto_ref, dqo_ref, dko_ref, dvo_ref,
    own, back, total, done, local, mate_sems, blk_sems,
):
    me = lax.axis_index("blk")
    core = lax.axis_index("uly")
    mate = 1 - core
    rows, width = atto_ref.shape
    half, kv_half = width // 2, dko_ref.shape[1] // 2
    greet(shards, me, mate)

    def send(o):
        to = lax.rem(me + o, shards)
        return pltpu.make_async_remote_copy(
            src_ref=grad_ref.at[:, pl.ds(pl.multiple_of((qb + to * CAP) * BLOCK, BLOCK), CAP * BLOCK), :],
            dst_ref=back.at[o - 1],
            send_sem=blk_sems.at[0, o - 1],
            recv_sem=blk_sems.at[1, o - 1],
            device_id={"blk": to},
            device_id_type=MESH,
        )

    def start(o, carry):
        send(o).start()
        return carry

    lax.fori_loop(1, shards, start, 0)
    mine = pltpu.make_async_copy(grad_ref.at[:, pl.ds(0, qb * BLOCK), :], own, local.at[0])
    mine.start()
    there = part(core, half)
    ats = to_mate(att_ref.at[part(mate, rows), :], atto_ref.at[:, there], mate_sems, 0, mate)
    dqs = to_mate(dq_ref.at[part(mate, rows), :], dqo_ref.at[:, there], mate_sems, 1, mate)
    ats.start()
    dqs.start()
    atl = pltpu.make_async_copy(att_ref.at[part(core, rows), :], atto_ref.at[:, there], local.at[1])
    dql = pltpu.make_async_copy(dq_ref.at[part(core, rows), :], dqo_ref.at[:, there], local.at[2])
    atl.start()
    dql.start()
    mine.wait()
    total[...] = own[...].astype(jnp.float32)

    def add(o, carry):
        send(o).wait()
        source = lax.rem(me - o + shards, shards)
        for l in range(qb):
            lo = l * BLOCK
            pick = sel_ref[source * qb + l]
            for t in range(2):
                term = total[t, lo:lo + BLOCK, :]
                for s in range(CAP):
                    piece = back[o - 1, t, s * BLOCK:(s + 1) * BLOCK, :].astype(jnp.float32)
                    term = term + jnp.where(pick == s, piece, 0.0)
                total[t, lo:lo + BLOCK, :] = term
        return carry

    lax.fori_loop(1, shards, add, 0)
    done[...] = total[...].astype(done.dtype)
    kv_there = part(core, kv_half)
    kvs = []
    for t, ref in enumerate((dko_ref, dvo_ref)):
        kvs.append(to_mate(done.at[t, part(mate, rows), :], ref.at[:, kv_there], mate_sems, 2 + t, mate))
        kvs.append(pltpu.make_async_copy(done.at[t, part(core, rows), :], ref.at[:, kv_there], local.at[3 + t]))
    for copy in kvs:
        copy.start()
    ats.wait()
    dqs.wait()
    atl.wait()
    dql.wait()
    for copy in kvs:
        copy.wait()


def give_call(sel, att, dq, grads, shards, qb):
    tokens, half = att.shape
    rows, kv_half = tokens // 2, grads.shape[2]
    wide = jax.ShapeDtypeStruct((rows, 2 * half), att.dtype)
    narrow = jax.ShapeDtypeStruct((rows, 2 * kv_half), att.dtype)
    return pl.pallas_call(
        functools.partial(give, shards, qb),
        out_shape=(wide, wide, narrow, narrow),
        in_specs=[SMEM, ANY, ANY, ANY],
        out_specs=(ANY, ANY, ANY, ANY),
        scratch_shapes=[
            pltpu.VMEM((2, qb * BLOCK, kv_half), jnp.bfloat16),
            pltpu.VMEM((shards - 1, 2, CAP * BLOCK, kv_half), jnp.bfloat16),
            pltpu.VMEM((2, qb * BLOCK, kv_half), jnp.float32),
            pltpu.VMEM((2, qb * BLOCK, kv_half), jnp.bfloat16),
            pltpu.SemaphoreType.DMA((5,)),
            pltpu.SemaphoreType.DMA((2, 4)),
            pltpu.SemaphoreType.DMA((2, shards - 1)),
        ],
        compiler_params=pltpu.CompilerParams(
            collective_id=1, has_side_effects=True, vmem_limit_bytes=40 * 1024 * 1024
        ),
        name="give",
    )(sel, att, dq, grads)


def plan(pattern, position, shards, qb):
    blocks, kb = pattern.shape
    ids = jnp.arange(blocks, dtype=jnp.int32)
    owner = ids // qb
    per_shard = pattern.reshape(shards, qb * kb)
    listed = jnp.any(per_shard[:, :, None] == ids[None, None, :], axis=1).astype(jnp.int32)
    before = ((owner[:, None] == owner[None, :]) & (ids[:, None] < ids[None, :])).astype(jnp.int32)
    rank_all = jnp.sum(listed[:, :, None] * before[None], axis=1)
    mine = lax.dynamic_slice_in_dim(per_shard, position, 1, 0).reshape(-1)
    my_rank = lax.dynamic_slice_in_dim(rank_all, position, 1, 0)
    rank = jnp.sum(jnp.where(mine[:, None] == ids[None, :], my_rank, 0), axis=1)
    pool = jnp.where(mine // qb == position, mine % qb, qb + (mine // qb) * CAP + rank)
    ranked = jnp.where(listed > 0, rank_all, -1)
    slots = jnp.arange(CAP, dtype=jnp.int32)
    within = jnp.arange(qb, dtype=jnp.int32)

    def table(owner_at):
        pick = lax.dynamic_slice_in_dim(ranked, owner_at * qb, qb, 1)
        idx = jnp.sum(jnp.where(pick[:, None, :] == slots[None, :, None], within, 0), axis=2)
        return pick, idx.reshape(-1)

    pick, near = table(position)
    far = table((position + shards // 2) % shards)[1]
    return pool, jnp.concatenate([near, far]), pick.reshape(-1)


def on_device(queries, key_states, value_states, out_grad, pattern):
    shards = lax.axis_size("blk")
    position = lax.axis_index("blk")
    qb = 2 * queries.shape[0] // BLOCK
    kb = pattern.shape[1]
    pool_size = qb + shards * CAP
    pool, idx, pick = plan(pattern, position, shards, qb)
    q, do, kv = bring_call(idx, queries, out_grad, key_states, value_states, shards, qb, pool_size)
    att, dq, grads = attend_call(pool, pool, q, do, kv, qb, kb, pool_size)
    return give_call(pick, att, dq, grads, shards, qb)


def solution(mesh):
    split = P(("group", "blk", "uly"), None)
    return jax.shard_map(
        on_device,
        mesh=mesh,
        in_specs=(split, split, split, split, P()),
        out_specs=(split, split, split, split),
        check_vma=False,
    )
```

```python
import functools
import math

import jax
import jax.numpy as jnp
from jax import lax
from jax.experimental import pallas as pl
from jax.experimental.pallas import tpu as pltpu
from jax.sharding import PartitionSpec as P

HD = 128
BLOCK = 64
CAP = 2


def dot(a, b, dims):
    return lax.dot_general(a, b, (dims, ((), ())), preferred_element_type=jnp.float32)


def attend(
    repeat, qb, kb, rows_ref, pool_ref, q_ref, do_ref, k_ref, v_ref,
    att_ref, dq_ref, grad_ref, kl, vl, acc_k, acc_v,
):
    scale = HD ** (-0.5)
    acc_k[...] = jnp.zeros_like(acc_k)
    acc_v[...] = jnp.zeros_like(acc_v)
    for i in range(qb):
        tokens = pl.ds(i * BLOCK, BLOCK)
        for c in range(kb):
            row = pl.multiple_of(rows_ref[i * kb + c] * BLOCK, BLOCK)
            kl[pl.ds(c * BLOCK, BLOCK), :] = k_ref[pl.ds(row, BLOCK), :]
            vl[pl.ds(c * BLOCK, BLOCK), :] = v_ref[pl.ds(row, BLOCK), :]
        q = jnp.concatenate([q_ref[tokens, r * HD:(r + 1) * HD] for r in range(repeat)], axis=0)
        do = jnp.concatenate([do_ref[tokens, r * HD:(r + 1) * HD] for r in range(repeat)], axis=0)
        k = kl[...]
        v = vl[...]
        s = dot(k, q, ((1,), (1,))) * (scale * math.log2(math.e))
        e = jnp.exp2(s - jnp.max(s, axis=0, keepdims=True))
        p = e * (1.0 / jnp.sum(e, axis=0, keepdims=True))
        p_low = p.astype(jnp.bfloat16)
        att = dot(v, p_low, ((0,), (0,))).astype(jnp.bfloat16)
        do_t = jnp.transpose(do.astype(jnp.float32))
        delta = jnp.sum(do_t * att.astype(jnp.float32), axis=0, keepdims=True)
        dp = dot(v, do, ((1,), (1,)))
        ds_low = (p * (dp - delta)).astype(jnp.bfloat16)
        dq = dot(k, ds_low, ((0,), (0,))) * scale
        dk = dot(ds_low, q, ((1,), (0,))) * scale
        dv = dot(p_low, do, ((1,), (0,)))
        att_n = jnp.transpose(att.astype(jnp.float32)).astype(jnp.bfloat16)
        dq_n = jnp.transpose(dq).astype(jnp.bfloat16)
        for r in range(repeat):
            att_ref[tokens, r * HD:(r + 1) * HD] = att_n[r * BLOCK:(r + 1) * BLOCK]
            dq_ref[tokens, r * HD:(r + 1) * HD] = dq_n[r * BLOCK:(r + 1) * BLOCK]
        for c in range(kb):
            at = pl.ds(pl.multiple_of(pool_ref[i * kb + c] * BLOCK, BLOCK), BLOCK)
            acc_k[at, :] += dk[c * BLOCK:(c + 1) * BLOCK]
            acc_v[at, :] += dv[c * BLOCK:(c + 1) * BLOCK]
    grad_ref[0] = acc_k[...].astype(jnp.bfloat16)
    grad_ref[1] = acc_v[...].astype(jnp.bfloat16)


def attend_call(rows, pool, q, do, kv, qb, kb, pool_size):
    tokens, width = q.shape
    kv_rows, kv2 = kv.shape
    groups = kv2 // 2 // HD
    cols = width // groups
    q_spec = pl.BlockSpec((tokens, cols), lambda g, *_: (0, g))
    pr = pool_size * BLOCK
    return pl.pallas_call(
        functools.partial(attend, cols // HD, qb, kb),
        out_shape=(
            jax.ShapeDtypeStruct((tokens, width), jnp.bfloat16),
            jax.ShapeDtypeStruct((tokens, width), jnp.bfloat16),
            jax.ShapeDtypeStruct((2, pr, kv2 // 2), jnp.bfloat16),
        ),
        grid_spec=pltpu.PrefetchScalarGridSpec(
            num_scalar_prefetch=2,
            grid=(groups,),
            in_specs=[
                q_spec,
                q_spec,
                pl.BlockSpec((kv_rows, HD), lambda g, *_: (0, g)),
                pl.BlockSpec((kv_rows, HD), lambda g, *_: (0, groups + g)),
            ],
            out_specs=[q_spec, q_spec, pl.BlockSpec((2, pr, HD), lambda g, *_: (0, 0, g))],
            scratch_shapes=[
                pltpu.VMEM((kb * BLOCK, HD), jnp.bfloat16),
                pltpu.VMEM((kb * BLOCK, HD), jnp.bfloat16),
                pltpu.VMEM((pr, HD), jnp.float32),
                pltpu.VMEM((pr, HD), jnp.float32),
            ],
        ),
        compiler_params=pltpu.CompilerParams(vmem_limit_bytes=56 * 1024 * 1024),
        name="attend",
    )(rows, pool, q, do, kv, kv)


MESH = pl.DeviceIdType.MESH
ANY = pl.BlockSpec(memory_space=pl.ANY)
SMEM = pl.BlockSpec(memory_space=pltpu.SMEM)


def part(index, size):
    return pl.ds(pl.multiple_of(index * size, size), size)


def greet(shards, me, mate):
    barrier = pltpu.get_barrier_semaphore()
    pl.semaphore_signal(barrier, inc=1, device_id={"uly": mate}, device_id_type=MESH)

    def one(o, carry):
        pl.semaphore_signal(
            barrier, inc=1, device_id={"blk": lax.rem(me + o, shards)}, device_id_type=MESH
        )
        return carry

    lax.fori_loop(1, shards, one, 0)
    pl.semaphore_wait(barrier, shards)


def to_mate(src, dst, sems, at, mate):
    return pltpu.make_async_remote_copy(
        src_ref=src, dst_ref=dst, send_sem=sems.at[0, at], recv_sem=sems.at[1, at],
        device_id={"uly": mate}, device_id_type=MESH,
    )


def bring(
    shards, qb, idx_ref, q_ref, do_ref, k_ref, v_ref, qh_ref, doh_ref, pool_ref,
    kv, far, out, local, mate_sems, twin_sems, blk_sems,
):
    me = lax.axis_index("blk")
    core = lax.axis_index("uly")
    mate = 1 - core
    rows, width = q_ref.shape
    half, kv_half = width // 2, k_ref.shape[1] // 2
    here = part(core, rows)
    first = pl.ds(0, kv_half)
    second = pl.ds(kv_half, kv_half)
    greet(shards, me, mate)
    ks = to_mate(k_ref.at[:, part(mate, kv_half)], kv.at[here, first], mate_sems, 0, mate)
    vs = to_mate(v_ref.at[:, part(mate, kv_half)], kv.at[here, second], mate_sems, 1, mate)
    ks.start()
    vs.start()
    kl = pltpu.make_async_copy(k_ref.at[:, part(core, kv_half)], kv.at[here, first], local.at[0])
    vl = pltpu.make_async_copy(v_ref.at[:, part(core, kv_half)], kv.at[here, second], local.at[1])
    kl.start()
    vl.start()
    kl.wait()
    vl.wait()
    ks.wait()
    vs.wait()

    half_size = shards // 2
    base = me // half_size * half_size
    place = lax.rem(me, half_size)
    twin = lax.rem(me + half_size, shards)
    halves = (first, second)

    def relay(t):
        return pltpu.make_async_remote_copy(
            src_ref=kv.at[:, halves[t]],
            dst_ref=far.at[:, halves[t]],
            send_sem=twin_sems.at[0, t],
            recv_sem=twin_sems.at[1, t],
            device_id={"blk": twin},
            device_id_type=MESH,
        )

    def send(f, t, o):
        owner = twin if f else me
        return pltpu.make_async_remote_copy(
            src_ref=out.at[f, o, :, halves[t]],
            dst_ref=pool_ref.at[
                pl.ds(pl.multiple_of((qb + owner * CAP) * BLOCK, BLOCK), CAP * BLOCK), halves[t]
            ],
            send_sem=blk_sems.at[0, f, t, o],
            recv_sem=blk_sems.at[1, f, t, o],
            device_id={"blk": base + lax.rem(place + o, half_size)},
            device_id_type=MESH,
        )

    def pack(source, f, t, o):
        to = base + lax.rem(place + o, half_size)
        for s in range(CAP):
            which = idx_ref[(f * shards + to) * CAP + s]
            block = source[0:BLOCK, halves[t]]
            for b in range(1, qb):
                block = jnp.where(which == b, source[b * BLOCK:(b + 1) * BLOCK, halves[t]], block)
            out[f, o, s * BLOCK:(s + 1) * BLOCK, halves[t]] = block

    relay(0).start()
    relay(1).start()

    def near(o, carry):
        for t in range(2):
            pack(kv, 0, t, o)
            send(0, t, o).start()
        return carry

    lax.fori_loop(1, half_size, near, 0)
    own = pltpu.make_async_copy(kv, pool_ref.at[pl.ds(0, qb * BLOCK), :], local.at[0])
    own.start()
    qs = to_mate(q_ref.at[:, part(mate, half)], qh_ref.at[here, :], mate_sems, 2, mate)
    ds = to_mate(do_ref.at[:, part(mate, half)], doh_ref.at[here, :], mate_sems, 3, mate)
    qs.start()
    ds.start()
    ql = pltpu.make_async_copy(q_ref.at[:, part(core, half)], qh_ref.at[here, :], local.at[1])
    dl = pltpu.make_async_copy(do_ref.at[:, part(core, half)], doh_ref.at[here, :], local.at[2])
    ql.start()
    dl.start()
    for t in range(2):
        relay(t).wait()

        def onward(o, carry):
            pack(far, 1, t, o)
            send(1, t, o).start()
            return carry

        lax.fori_loop(1, half_size, onward, 0)
        pack(far, 1, t, 0)
    kept = pltpu.make_async_copy(
        out.at[1, 0],
        pool_ref.at[pl.ds(pl.multiple_of((qb + twin * CAP) * BLOCK, BLOCK), CAP * BLOCK), :],
        local.at[3],
    )
    kept.start()
    own.wait()
    ql.wait()
    dl.wait()
    qs.wait()
    ds.wait()
    kept.wait()

    def finish(o, carry):
        for f in range(2):
            for t in range(2):
                send(f, t, o).wait()
        return carry

    lax.fori_loop(1, half_size, finish, 0)


def bring_call(idx, q, do, k, v, shards, qb, pool_size):
    rows, width = q.shape
    kv_width = k.shape[1]
    heads = jax.ShapeDtypeStruct((2 * rows, width // 2), q.dtype)
    return pl.pallas_call(
        functools.partial(bring, shards, qb),
        out_shape=(heads, heads, jax.ShapeDtypeStruct((pool_size * BLOCK, kv_width), k.dtype)),
        in_specs=[SMEM, ANY, ANY, ANY, ANY],
        out_specs=(ANY, ANY, ANY),
        scratch_shapes=[
            pltpu.VMEM((qb * BLOCK, kv_width), k.dtype),
            pltpu.VMEM((qb * BLOCK, kv_width), k.dtype),
            pltpu.VMEM((2, shards // 2, CAP * BLOCK, kv_width), k.dtype),
            pltpu.SemaphoreType.DMA((4,)),
            pltpu.SemaphoreType.DMA((2, 4)),
            pltpu.SemaphoreType.DMA((2, 2)),
            pltpu.SemaphoreType.DMA((2, 2, 2, shards // 2)),
        ],
        compiler_params=pltpu.CompilerParams(
            collective_id=0, has_side_effects=True, vmem_limit_bytes=56 * 1024 * 1024
        ),
        name="bring",
    )(idx, q, do, k, v)


def give(
    shards, qb, sel_ref, att_ref, dq_ref, grad_ref, atto_ref, dqo_ref, dko_ref, dvo_ref,
    own, back, total, fold, low, relayed, done, local, mate_sems, twin_sems, blk_sems,
):
    me = lax.axis_index("blk")
    core = lax.axis_index("uly")
    mate = 1 - core
    rows, width = atto_ref.shape
    half, kv_half = width // 2, dko_ref.shape[1] // 2
    greet(shards, me, mate)

    half_size = shards // 2
    base = me // half_size * half_size
    place = lax.rem(me, half_size)
    twin = lax.rem(me + half_size, shards)

    def slots_of(owner):
        return pl.ds(pl.multiple_of((qb + owner * CAP) * BLOCK, BLOCK), CAP * BLOCK)

    def send(f, t, o):
        member = base + lax.rem(place + o, half_size)
        owner = lax.rem(member + half_size, shards) if f else member
        return pltpu.make_async_remote_copy(
            src_ref=grad_ref.at[t, slots_of(owner), :],
            dst_ref=back.at[f, t, o],
            send_sem=blk_sems.at[0, f, t, o],
            recv_sem=blk_sems.at[1, f, t, o],
            device_id={"blk": member},
            device_id_type=MESH,
        )

    def across(t):
        return pltpu.make_async_remote_copy(
            src_ref=low.at[t],
            dst_ref=relayed.at[t],
            send_sem=twin_sems.at[0, t],
            recv_sem=twin_sems.at[1, t],
            device_id={"blk": twin},
            device_id_type=MESH,
        )

    for f, t in ((1, 0), (1, 1), (0, 0), (0, 1)):

        def start(o, carry, f=f, t=t):
            send(f, t, o).start()
            return carry

        lax.fori_loop(1, half_size, start, 0)
    kept = [
        pltpu.make_async_copy(grad_ref.at[t, slots_of(twin), :], back.at[1, t, 0], local.at[5 + t])
        for t in range(2)
    ]
    kept[0].start()
    kept[1].start()
    mine = pltpu.make_async_copy(grad_ref.at[:, pl.ds(0, qb * BLOCK), :], own, local.at[0])
    mine.start()
    there = part(core, half)
    ats = to_mate(att_ref.at[part(mate, rows), :], atto_ref.at[:, there], mate_sems, 0, mate)
    dqs = to_mate(dq_ref.at[part(mate, rows), :], dqo_ref.at[:, there], mate_sems, 1, mate)
    ats.start()
    dqs.start()
    atl = pltpu.make_async_copy(att_ref.at[part(core, rows), :], atto_ref.at[:, there], local.at[1])
    dql = pltpu.make_async_copy(dq_ref.at[part(core, rows), :], dqo_ref.at[:, there], local.at[2])
    atl.start()
    dql.start()
    fold[...] = jnp.zeros_like(fold)

    def add(into, f, t, o):
        source = base + lax.rem(place - o + half_size, half_size)
        for l in range(qb):
            lo = l * BLOCK
            pick = sel_ref[(f * shards + source) * qb + l]
            term = into[t, lo:lo + BLOCK, :]
            for s in range(CAP):
                piece = back[f, t, o, s * BLOCK:(s + 1) * BLOCK, :].astype(jnp.float32)
                term = term + jnp.where(pick == s, piece, 0.0)
            into[t, lo:lo + BLOCK, :] = term

    for t in range(2):
        kept[t].wait()
        add(fold, 1, t, 0)

        def gather(o, carry, t=t):
            send(1, t, o).wait()
            add(fold, 1, t, o)
            return carry

        lax.fori_loop(1, half_size, gather, 0)
        low[t] = fold[t].astype(low.dtype)
        across(t).start()
    mine.wait()
    total[...] = own[...].astype(jnp.float32)
    for t in range(2):

        def near(o, carry, t=t):
            send(0, t, o).wait()
            add(total, 0, t, o)
            return carry

        lax.fori_loop(1, half_size, near, 0)
    kv_there = part(core, kv_half)
    kvs = []
    for t, ref in enumerate((dko_ref, dvo_ref)):
        across(t).wait()
        done[t] = (total[t] + relayed[t].astype(jnp.float32)).astype(done.dtype)
        kvs.append(to_mate(done.at[t, part(mate, rows), :], ref.at[:, kv_there], mate_sems, 2 + t, mate))
        kvs.append(pltpu.make_async_copy(done.at[t, part(core, rows), :], ref.at[:, kv_there], local.at[3 + t]))
        kvs[-2].start()
        kvs[-1].start()
    ats.wait()
    dqs.wait()
    atl.wait()
    dql.wait()
    for copy in kvs:
        copy.wait()


def give_call(sel, att, dq, grads, shards, qb):
    tokens, half = att.shape
    rows, kv_half = tokens // 2, grads.shape[2]
    wide = jax.ShapeDtypeStruct((rows, 2 * half), att.dtype)
    narrow = jax.ShapeDtypeStruct((rows, 2 * kv_half), att.dtype)
    return pl.pallas_call(
        functools.partial(give, shards, qb),
        out_shape=(wide, wide, narrow, narrow),
        in_specs=[SMEM, ANY, ANY, ANY],
        out_specs=(ANY, ANY, ANY, ANY),
        scratch_shapes=[
            pltpu.VMEM((2, qb * BLOCK, kv_half), jnp.bfloat16),
            pltpu.VMEM((2, 2, shards // 2, CAP * BLOCK, kv_half), jnp.bfloat16),
            pltpu.VMEM((2, qb * BLOCK, kv_half), jnp.float32),
            pltpu.VMEM((2, qb * BLOCK, kv_half), jnp.float32),
            pltpu.VMEM((2, qb * BLOCK, kv_half), jnp.bfloat16),
            pltpu.VMEM((2, qb * BLOCK, kv_half), jnp.bfloat16),
            pltpu.VMEM((2, qb * BLOCK, kv_half), jnp.bfloat16),
            pltpu.SemaphoreType.DMA((7,)),
            pltpu.SemaphoreType.DMA((2, 4)),
            pltpu.SemaphoreType.DMA((2, 2)),
            pltpu.SemaphoreType.DMA((2, 2, 2, shards // 2)),
        ],
        compiler_params=pltpu.CompilerParams(
            collective_id=1, has_side_effects=True, vmem_limit_bytes=40 * 1024 * 1024
        ),
        name="give",
    )(sel, att, dq, grads)


def plan(pattern, position, shards, qb):
    blocks, kb = pattern.shape
    ids = jnp.arange(blocks, dtype=jnp.int32)
    owner = ids // qb
    per_shard = pattern.reshape(shards, qb * kb)
    listed = jnp.any(per_shard[:, :, None] == ids[None, None, :], axis=1).astype(jnp.int32)
    before = ((owner[:, None] == owner[None, :]) & (ids[:, None] < ids[None, :])).astype(jnp.int32)
    rank_all = jnp.sum(listed[:, :, None] * before[None], axis=1)
    mine = lax.dynamic_slice_in_dim(per_shard, position, 1, 0).reshape(-1)
    my_rank = lax.dynamic_slice_in_dim(rank_all, position, 1, 0)
    rank = jnp.sum(jnp.where(mine[:, None] == ids[None, :], my_rank, 0), axis=1)
    pool = jnp.where(mine // qb == position, mine % qb, qb + (mine // qb) * CAP + rank)
    ranked = jnp.where(listed > 0, rank_all, -1)
    slots = jnp.arange(CAP, dtype=jnp.int32)
    within = jnp.arange(qb, dtype=jnp.int32)

    def table(owner_at):
        pick = lax.dynamic_slice_in_dim(ranked, owner_at * qb, qb, 1)
        idx = jnp.sum(jnp.where(pick[:, None, :] == slots[None, :, None], within, 0), axis=2)
        return pick, idx.reshape(-1)

    pick, near = table(position)
    far_pick, far = table((position + shards // 2) % shards)
    pick = jnp.concatenate([pick.reshape(-1), far_pick.reshape(-1)])
    return pool, jnp.concatenate([near, far]), pick


def on_device(queries, key_states, value_states, out_grad, pattern):
    shards = lax.axis_size("blk")
    position = lax.axis_index("blk")
    qb = 2 * queries.shape[0] // BLOCK
    kb = pattern.shape[1]
    pool_size = qb + shards * CAP
    pool, idx, pick = plan(pattern, position, shards, qb)
    q, do, kv = bring_call(idx, queries, out_grad, key_states, value_states, shards, qb, pool_size)
    att, dq, grads = attend_call(pool, pool, q, do, kv, qb, kb, pool_size)
    return give_call(pick, att, dq, grads, shards, qb)


def solution(mesh):
    split = P(("group", "blk", "uly"), None)
    return jax.shard_map(
        on_device,
        mesh=mesh,
        in_specs=(split, split, split, split, P()),
        out_specs=(split, split, split, split),
        check_vma=False,
    )
```

```python
import functools
import math

import jax
import jax.numpy as jnp
from jax import lax
from jax.experimental import pallas as pl
from jax.experimental.pallas import tpu as pltpu
from jax.sharding import PartitionSpec as P

HD = 128
BLOCK = 64
CAP = 2


def dot(a, b, dims):
    return lax.dot_general(a, b, (dims, ((), ())), preferred_element_type=jnp.float32)


def attend(
    repeat, qb, kb, rows_ref, pool_ref, q_ref, do_ref, k_ref, v_ref,
    att_ref, dq_ref, grad_ref, kl, vl, acc_k, acc_v,
):
    scale = HD ** (-0.5)
    acc_k[...] = jnp.zeros_like(acc_k)
    acc_v[...] = jnp.zeros_like(acc_v)
    for i in range(qb):
        tokens = pl.ds(i * BLOCK, BLOCK)
        for c in range(kb):
            row = pl.multiple_of(rows_ref[i * kb + c] * BLOCK, BLOCK)
            kl[pl.ds(c * BLOCK, BLOCK), :] = k_ref[pl.ds(row, BLOCK), :]
            vl[pl.ds(c * BLOCK, BLOCK), :] = v_ref[pl.ds(row, BLOCK), :]
        q = jnp.concatenate([q_ref[tokens, r * HD:(r + 1) * HD] for r in range(repeat)], axis=0)
        do = jnp.concatenate([do_ref[tokens, r * HD:(r + 1) * HD] for r in range(repeat)], axis=0)
        k = kl[...]
        v = vl[...]
        s = dot(k, q, ((1,), (1,))) * (scale * math.log2(math.e))
        e = jnp.exp2(s - jnp.max(s, axis=0, keepdims=True))
        p = e * (1.0 / jnp.sum(e, axis=0, keepdims=True))
        p_low = p.astype(jnp.bfloat16)
        att = dot(v, p_low, ((0,), (0,))).astype(jnp.bfloat16)
        do_t = jnp.transpose(do.astype(jnp.float32))
        delta = jnp.sum(do_t * att.astype(jnp.float32), axis=0, keepdims=True)
        dp = dot(v, do, ((1,), (1,)))
        ds_low = (p * (dp - delta)).astype(jnp.bfloat16)
        dq = dot(k, ds_low, ((0,), (0,))) * scale
        dk = dot(ds_low, q, ((1,), (0,))) * scale
        dv = dot(p_low, do, ((1,), (0,)))
        att_n = jnp.transpose(att.astype(jnp.float32)).astype(jnp.bfloat16)
        dq_n = jnp.transpose(dq).astype(jnp.bfloat16)
        for r in range(repeat):
            att_ref[tokens, r * HD:(r + 1) * HD] = att_n[r * BLOCK:(r + 1) * BLOCK]
            dq_ref[tokens, r * HD:(r + 1) * HD] = dq_n[r * BLOCK:(r + 1) * BLOCK]
        for c in range(kb):
            at = pl.ds(pl.multiple_of(pool_ref[i * kb + c] * BLOCK, BLOCK), BLOCK)
            acc_k[at, :] += dk[c * BLOCK:(c + 1) * BLOCK]
            acc_v[at, :] += dv[c * BLOCK:(c + 1) * BLOCK]
    grad_ref[0] = acc_k[...].astype(jnp.bfloat16)
    grad_ref[1] = acc_v[...].astype(jnp.bfloat16)


def attend_call(rows, pool, q, do, kv, qb, kb, pool_size):
    tokens, width = q.shape
    kv_rows, kv2 = kv.shape
    groups = kv2 // 2 // HD
    cols = width // groups
    q_spec = pl.BlockSpec((tokens, cols), lambda g, *_: (0, g))
    pr = pool_size * BLOCK
    return pl.pallas_call(
        functools.partial(attend, cols // HD, qb, kb),
        out_shape=(
            jax.ShapeDtypeStruct((tokens, width), jnp.bfloat16),
            jax.ShapeDtypeStruct((tokens, width), jnp.bfloat16),
            jax.ShapeDtypeStruct((2, pr, kv2 // 2), jnp.bfloat16),
        ),
        grid_spec=pltpu.PrefetchScalarGridSpec(
            num_scalar_prefetch=2,
            grid=(groups,),
            in_specs=[
                q_spec,
                q_spec,
                pl.BlockSpec((kv_rows, HD), lambda g, *_: (0, g)),
                pl.BlockSpec((kv_rows, HD), lambda g, *_: (0, groups + g)),
            ],
            out_specs=[q_spec, q_spec, pl.BlockSpec((2, pr, HD), lambda g, *_: (0, 0, g))],
            scratch_shapes=[
                pltpu.VMEM((kb * BLOCK, HD), jnp.bfloat16),
                pltpu.VMEM((kb * BLOCK, HD), jnp.bfloat16),
                pltpu.VMEM((pr, HD), jnp.float32),
                pltpu.VMEM((pr, HD), jnp.float32),
            ],
        ),
        compiler_params=pltpu.CompilerParams(vmem_limit_bytes=56 * 1024 * 1024),
        name="attend",
    )(rows, pool, q, do, kv, kv)


MESH = pl.DeviceIdType.MESH
ANY = pl.BlockSpec(memory_space=pl.ANY)
SMEM = pl.BlockSpec(memory_space=pltpu.SMEM)


def part(index, size):
    return pl.ds(pl.multiple_of(index * size, size), size)


def greet(shards, me, mate):
    barrier = pltpu.get_barrier_semaphore()
    pl.semaphore_signal(barrier, inc=1, device_id={"uly": mate}, device_id_type=MESH)

    def one(o, carry):
        pl.semaphore_signal(
            barrier, inc=1, device_id={"blk": lax.rem(me + o, shards)}, device_id_type=MESH
        )
        return carry

    lax.fori_loop(1, shards, one, 0)
    pl.semaphore_wait(barrier, shards)


def to_mate(src, dst, sems, at, mate):
    return pltpu.make_async_remote_copy(
        src_ref=src, dst_ref=dst, send_sem=sems.at[0, at], recv_sem=sems.at[1, at],
        device_id={"uly": mate}, device_id_type=MESH,
    )


def bring(
    shards, qb, idx_ref, q_ref, do_ref, k_ref, v_ref, qh_ref, doh_ref, pool_ref,
    kv, far, out, local, mate_sems, twin_sems, blk_sems,
):
    me = lax.axis_index("blk")
    core = lax.axis_index("uly")
    mate = 1 - core
    rows, width = q_ref.shape
    half, kv_half = width // 2, k_ref.shape[1] // 2
    here = part(core, rows)
    first = pl.ds(0, kv_half)
    second = pl.ds(kv_half, kv_half)
    greet(shards, me, mate)
    ks = to_mate(k_ref.at[:, part(mate, kv_half)], kv.at[here, first], mate_sems, 0, mate)
    vs = to_mate(v_ref.at[:, part(mate, kv_half)], kv.at[here, second], mate_sems, 1, mate)
    ks.start()
    vs.start()
    kl = pltpu.make_async_copy(k_ref.at[:, part(core, kv_half)], kv.at[here, first], local.at[0])
    vl = pltpu.make_async_copy(v_ref.at[:, part(core, kv_half)], kv.at[here, second], local.at[1])
    kl.start()
    vl.start()
    kl.wait()
    vl.wait()
    ks.wait()
    vs.wait()

    half_size = shards // 2
    base = me // half_size * half_size
    place = lax.rem(me, half_size)
    twin = lax.rem(me + half_size, shards)
    halves = (first, second)

    def relay(t):
        return pltpu.make_async_remote_copy(
            src_ref=kv.at[:, halves[t]],
            dst_ref=far.at[:, halves[t]],
            send_sem=twin_sems.at[0, t],
            recv_sem=twin_sems.at[1, t],
            device_id={"blk": twin},
            device_id_type=MESH,
        )

    def send(f, t, o):
        owner = twin if f else me
        return pltpu.make_async_remote_copy(
            src_ref=out.at[f, o, :, halves[t]],
            dst_ref=pool_ref.at[
                pl.ds(pl.multiple_of((qb + owner * CAP) * BLOCK, BLOCK), CAP * BLOCK), halves[t]
            ],
            send_sem=blk_sems.at[0, f, t, o],
            recv_sem=blk_sems.at[1, f, t, o],
            device_id={"blk": base + lax.rem(place + o, half_size)},
            device_id_type=MESH,
        )

    def pack(source, f, t, o):
        to = base + lax.rem(place + o, half_size)
        for s in range(CAP):
            which = idx_ref[(f * shards + to) * CAP + s]
            block = source[0:BLOCK, halves[t]]
            for b in range(1, qb):
                block = jnp.where(which == b, source[b * BLOCK:(b + 1) * BLOCK, halves[t]], block)
            out[f, o, s * BLOCK:(s + 1) * BLOCK, halves[t]] = block

    relay(0).start()
    relay(1).start()

    def near(o, carry):
        for t in range(2):
            pack(kv, 0, t, o)
            send(0, t, o).start()
        return carry

    lax.fori_loop(1, half_size, near, 0)
    own = pltpu.make_async_copy(kv, pool_ref.at[pl.ds(0, qb * BLOCK), :], local.at[0])
    own.start()
    qs = to_mate(q_ref.at[:, part(mate, half)], qh_ref.at[here, :], mate_sems, 2, mate)
    ds = to_mate(do_ref.at[:, part(mate, half)], doh_ref.at[here, :], mate_sems, 3, mate)
    qs.start()
    ds.start()
    ql = pltpu.make_async_copy(q_ref.at[:, part(core, half)], qh_ref.at[here, :], local.at[1])
    dl = pltpu.make_async_copy(do_ref.at[:, part(core, half)], doh_ref.at[here, :], local.at[2])
    ql.start()
    dl.start()
    for t in range(2):
        relay(t).wait()

        def onward(o, carry):
            pack(far, 1, t, o)
            send(1, t, o).start()
            return carry

        lax.fori_loop(1, half_size, onward, 0)
        pack(far, 1, t, 0)
    kept = pltpu.make_async_copy(
        out.at[1, 0],
        pool_ref.at[pl.ds(pl.multiple_of((qb + twin * CAP) * BLOCK, BLOCK), CAP * BLOCK), :],
        local.at[3],
    )
    kept.start()
    own.wait()
    ql.wait()
    dl.wait()
    qs.wait()
    ds.wait()
    kept.wait()

    def finish(o, carry):
        for f in range(2):
            for t in range(2):
                send(f, t, o).wait()
        return carry

    lax.fori_loop(1, half_size, finish, 0)


def bring_call(idx, q, do, k, v, shards, qb, pool_size):
    rows, width = q.shape
    kv_width = k.shape[1]
    heads = jax.ShapeDtypeStruct((2 * rows, width // 2), q.dtype)
    return pl.pallas_call(
        functools.partial(bring, shards, qb),
        out_shape=(heads, heads, jax.ShapeDtypeStruct((pool_size * BLOCK, kv_width), k.dtype)),
        in_specs=[SMEM, ANY, ANY, ANY, ANY],
        out_specs=(ANY, ANY, ANY),
        scratch_shapes=[
            pltpu.VMEM((qb * BLOCK, kv_width), k.dtype),
            pltpu.VMEM((qb * BLOCK, kv_width), k.dtype),
            pltpu.VMEM((2, shards // 2, CAP * BLOCK, kv_width), k.dtype),
            pltpu.SemaphoreType.DMA((4,)),
            pltpu.SemaphoreType.DMA((2, 4)),
            pltpu.SemaphoreType.DMA((2, 2)),
            pltpu.SemaphoreType.DMA((2, 2, 2, shards // 2)),
        ],
        compiler_params=pltpu.CompilerParams(
            collective_id=0, has_side_effects=True, vmem_limit_bytes=56 * 1024 * 1024
        ),
        name="bring",
    )(idx, q, do, k, v)


def give(
    shards, qb, sel_ref, att_ref, dq_ref, grad_ref, atto_ref, dqo_ref, dko_ref, dvo_ref,
    own, back, total, fold, low, relayed, done, local, mate_sems, twin_sems, blk_sems,
):
    me = lax.axis_index("blk")
    core = lax.axis_index("uly")
    mate = 1 - core
    rows, width = atto_ref.shape
    half, kv_half = width // 2, dko_ref.shape[1] // 2
    greet(shards, me, mate)

    half_size = shards // 2
    base = me // half_size * half_size
    place = lax.rem(me, half_size)
    twin = lax.rem(me + half_size, shards)

    def slots_of(owner):
        return pl.ds(pl.multiple_of((qb + owner * CAP) * BLOCK, BLOCK), CAP * BLOCK)

    def send(f, t, o):
        member = base + lax.rem(place + o, half_size)
        owner = lax.rem(member + half_size, shards) if f else member
        return pltpu.make_async_remote_copy(
            src_ref=grad_ref.at[t, slots_of(owner), :],
            dst_ref=back.at[f, t, o],
            send_sem=blk_sems.at[0, f, t, o],
            recv_sem=blk_sems.at[1, f, t, o],
            device_id={"blk": member},
            device_id_type=MESH,
        )

    def across(t):
        return pltpu.make_async_remote_copy(
            src_ref=low.at[t],
            dst_ref=relayed.at[t],
            send_sem=twin_sems.at[0, t],
            recv_sem=twin_sems.at[1, t],
            device_id={"blk": twin},
            device_id_type=MESH,
        )

    for f, t in ((1, 0), (1, 1), (0, 0), (0, 1)):

        def start(o, carry, f=f, t=t):
            send(f, t, o).start()
            return carry

        lax.fori_loop(1, half_size, start, 0)
    kept = [
        pltpu.make_async_copy(grad_ref.at[t, slots_of(twin), :], back.at[1, t, 0], local.at[5 + t])
        for t in range(2)
    ]
    kept[0].start()
    kept[1].start()
    mine = pltpu.make_async_copy(grad_ref.at[:, pl.ds(0, qb * BLOCK), :], own, local.at[0])
    mine.start()
    there = part(core, half)
    ats = to_mate(att_ref.at[part(mate, rows), :], atto_ref.at[:, there], mate_sems, 0, mate)
    dqs = to_mate(dq_ref.at[part(mate, rows), :], dqo_ref.at[:, there], mate_sems, 1, mate)
    ats.start()
    dqs.start()
    atl = pltpu.make_async_copy(att_ref.at[part(core, rows), :], atto_ref.at[:, there], local.at[1])
    dql = pltpu.make_async_copy(dq_ref.at[part(core, rows), :], dqo_ref.at[:, there], local.at[2])
    atl.start()
    dql.start()
    fold[...] = jnp.zeros_like(fold)

    def add(into, f, t, o):
        source = base + lax.rem(place - o + half_size, half_size)
        for l in range(qb):
            lo = l * BLOCK
            pick = sel_ref[(f * shards + source) * qb + l]
            term = into[t, lo:lo + BLOCK, :]
            for s in range(CAP):
                piece = back[f, t, o, s * BLOCK:(s + 1) * BLOCK, :].astype(jnp.float32)
                term = term + jnp.where(pick == s, piece, 0.0)
            into[t, lo:lo + BLOCK, :] = term

    for t in range(2):
        kept[t].wait()
        add(fold, 1, t, 0)

        def gather(o, carry, t=t):
            send(1, t, o).wait()
            add(fold, 1, t, o)
            return carry

        lax.fori_loop(1, half_size, gather, 0)
        low[t] = fold[t].astype(low.dtype)
        across(t).start()
    mine.wait()
    total[...] = own[...].astype(jnp.float32)
    for t in range(2):

        def near(o, carry, t=t):
            send(0, t, o).wait()
            add(total, 0, t, o)
            return carry

        lax.fori_loop(1, half_size, near, 0)
    kv_there = part(core, kv_half)
    kvs = []
    for t, ref in enumerate((dko_ref, dvo_ref)):
        across(t).wait()
        done[t] = (total[t] + relayed[t].astype(jnp.float32)).astype(done.dtype)
        kvs.append(to_mate(done.at[t, part(mate, rows), :], ref.at[:, kv_there], mate_sems, 2 + t, mate))
        kvs.append(pltpu.make_async_copy(done.at[t, part(core, rows), :], ref.at[:, kv_there], local.at[3 + t]))
        kvs[-2].start()
        kvs[-1].start()
    ats.wait()
    dqs.wait()
    atl.wait()
    dql.wait()
    for copy in kvs:
        copy.wait()


def give_call(sel, att, dq, grads, shards, qb):
    tokens, half = att.shape
    rows, kv_half = tokens // 2, grads.shape[2]
    wide = jax.ShapeDtypeStruct((rows, 2 * half), att.dtype)
    narrow = jax.ShapeDtypeStruct((rows, 2 * kv_half), att.dtype)
    return pl.pallas_call(
        functools.partial(give, shards, qb),
        out_shape=(wide, wide, narrow, narrow),
        in_specs=[SMEM, ANY, ANY, ANY],
        out_specs=(ANY, ANY, ANY, ANY),
        scratch_shapes=[
            pltpu.VMEM((2, qb * BLOCK, kv_half), jnp.bfloat16),
            pltpu.VMEM((2, 2, shards // 2, CAP * BLOCK, kv_half), jnp.bfloat16),
            pltpu.VMEM((2, qb * BLOCK, kv_half), jnp.float32),
            pltpu.VMEM((2, qb * BLOCK, kv_half), jnp.float32),
            pltpu.VMEM((2, qb * BLOCK, kv_half), jnp.bfloat16),
            pltpu.VMEM((2, qb * BLOCK, kv_half), jnp.bfloat16),
            pltpu.VMEM((2, qb * BLOCK, kv_half), jnp.bfloat16),
            pltpu.SemaphoreType.DMA((7,)),
            pltpu.SemaphoreType.DMA((2, 4)),
            pltpu.SemaphoreType.DMA((2, 2)),
            pltpu.SemaphoreType.DMA((2, 2, 2, shards // 2)),
        ],
        compiler_params=pltpu.CompilerParams(
            collective_id=1, has_side_effects=True, vmem_limit_bytes=56 * 1024 * 1024
        ),
        name="give",
    )(sel, att, dq, grads)


def plan(pattern, position, shards, qb):
    blocks, kb = pattern.shape
    ids = jnp.arange(blocks, dtype=jnp.int32)
    owner = ids // qb
    per_shard = pattern.reshape(shards, qb * kb)
    listed = jnp.any(per_shard[:, :, None] == ids[None, None, :], axis=1).astype(jnp.int32)
    before = ((owner[:, None] == owner[None, :]) & (ids[:, None] < ids[None, :])).astype(jnp.int32)
    rank_all = jnp.sum(listed[:, :, None] * before[None], axis=1)
    mine = lax.dynamic_slice_in_dim(per_shard, position, 1, 0).reshape(-1)
    my_rank = lax.dynamic_slice_in_dim(rank_all, position, 1, 0)
    rank = jnp.sum(jnp.where(mine[:, None] == ids[None, :], my_rank, 0), axis=1)
    pool = jnp.where(mine // qb == position, mine % qb, qb + (mine // qb) * CAP + rank)
    ranked = jnp.where(listed > 0, rank_all, -1)
    slots = jnp.arange(CAP, dtype=jnp.int32)
    within = jnp.arange(qb, dtype=jnp.int32)

    def table(owner_at):
        pick = lax.dynamic_slice_in_dim(ranked, owner_at * qb, qb, 1)
        idx = jnp.sum(jnp.where(pick[:, None, :] == slots[None, :, None], within, 0), axis=2)
        return pick, idx.reshape(-1)

    pick, near = table(position)
    far_pick, far = table((position + shards // 2) % shards)
    pick = jnp.concatenate([pick.reshape(-1), far_pick.reshape(-1)])
    return pool, jnp.concatenate([near, far]), pick


def on_device(queries, key_states, value_states, out_grad, pattern):
    shards = lax.axis_size("blk")
    position = lax.axis_index("blk")
    qb = 2 * queries.shape[0] // BLOCK
    kb = pattern.shape[1]
    pool_size = qb + shards * CAP
    pool, idx, pick = plan(pattern, position, shards, qb)
    q, do, kv = bring_call(idx, queries, out_grad, key_states, value_states, shards, qb, pool_size)
    att, dq, grads = attend_call(pool, pool, q, do, kv, qb, kb, pool_size)
    return give_call(pick, att, dq, grads, shards, qb)


def solution(mesh):
    split = P(("group", "blk", "uly"), None)
    return jax.shard_map(
        on_device,
        mesh=mesh,
        in_specs=(split, split, split, split, P()),
        out_specs=(split, split, split, split),
        check_vma=False,
    )
```
